128 devices in a mesh: ctx: 64 (over x, z_lo, y, core), head: 2 (over z_hi).
Axes of the slice: x: 4, y: 4, z: 4 (z_hi: 2, z_lo: 2; z = z_hi * 2 + z_lo), core: 2. Of those that a mesh axis runs over, the one named last changes fastest.
Arguments:
- queries: bfloat16 [65536, 2048], P('ctx', 'head'), may hold values from -6 to 6
- key_rows: bfloat16 [65536, 1024], P('ctx'), may hold values from -6 to 6
- value_rows: bfloat16 [65536, 1024], P('ctx'), may hold values from -6 to 6
- out_grad: bfloat16 [65536, 2048], P('ctx', 'head'), may hold values from -6 to 6
- doc_start: int32 [65536], P('ctx'), may hold values from 0 to 65535, as said below
Outputs:
- attended: bfloat16 [65536, 2048], P('ctx', 'head')
- query_grad: bfloat16 [65536, 2048], P('ctx', 'head')
- key_grad: bfloat16 [65536, 1024], P('ctx', 'head')
- value_grad: bfloat16 [65536, 1024], P('ctx', 'head')
The draws below stay inside these ranges and needn't reach their ends.
Inputs may be any that keep to these rules, and one draw needn't show every extreme that they name: `doc_start`: Non-decreasing; each value is at most its own position and equals it at a document's first position; position 0 starts a document, and the first document is longer than 1024 positions.
All inputs are finite; a program needn't handle non-finite values.
Results may differ from the reference program's by a relative error of at most 0.014.
Values may be sent and summed in bfloat16 or wider, within the bound.
No kernel may reach another device: no remote copies, remote signals or barrier semaphores. Data moves between devices by JAX's collectives and lax.ppermute only.
A program may use at most 192 MiB of HBM per device.

```python
import jax
import jax.numpy as jnp
from jax import lax

QH = 8
KVH = 4
HD = 256
WINDOW = 1024
TOK_DEV = 1024
TOKENS = 65536


def draw_queries(key, part):
    key = jax.random.fold_in(key, 1)
    return jnp.clip(jax.random.normal(key, (TOKENS, QH * HD), jnp.float32), -6.0, 6.0).astype(jnp.bfloat16)


def draw_key_rows(key, part):
    key = jax.random.fold_in(key, 2)
    return jnp.clip(jax.random.normal(key, (TOKENS, KVH * HD), jnp.float32), -6.0, 6.0).astype(jnp.bfloat16)


def draw_doc_start(key, part):
    key = jax.random.fold_in(key, 5)
    exponent = jax.random.randint(jax.random.fold_in(key, 1), (TOKENS // TOK_DEV,), 0, 7)
    threshold = jnp.left_shift(jnp.ones_like(exponent), exponent)
    positions = jnp.arange(TOKENS, dtype=jnp.int32)
    shard_ids = positions // TOK_DEV
    draws = jax.random.randint(jax.random.fold_in(key, 2), (TOKENS,), 0, 8 * TOK_DEV)
    forced = 2 * TOK_DEV + jax.random.randint(jax.random.fold_in(key, 3), (), 0, TOK_DEV)
    starts = (draws < threshold[shard_ids]) & (positions > TOK_DEV) | (positions == forced)
    starts = starts | (positions == 0)
    return lax.cummax(jnp.where(starts, positions, 0), axis=0).astype(jnp.int32)


def shard_levels(key, extent, cuts, least, top_value):
    loudness = 1.0
    for axis_at, blocks in cuts:
        steps = jax.random.uniform(jax.random.fold_in(jax.random.fold_in(key, 6), axis_at), (blocks,), jnp.float32, least / len(cuts), top_value / len(cuts))
        loudness = loudness * jnp.repeat(jnp.exp(steps), extent[axis_at] // blocks).reshape((-1,) + (1,) * (len(extent) - 1 - axis_at))
    return loudness


def centred(own_key, extent, width, bound, cuts=(), kind=jnp.bfloat16):
    array = jax.random.normal(own_key, extent, jnp.float32) * width
    if len(cuts) > 0:
        array = shard_levels(own_key, extent, cuts, -0.22, 0.18) * array
    return jnp.clip(array, min=-bound, max=bound).astype(kind)


def setup_inputs(seed: int = 0) -> dict:
    arg_keys = jax.random.split(jax.random.key(seed), 6)
    queries = draw_queries(jax.random.fold_in(arg_keys[5], 71), 0)
    key_rows = draw_key_rows(jax.random.fold_in(arg_keys[5], 71), 0)
    value_rows = centred(arg_keys[2], (TOKENS, KVH * HD), 1.0, 6.0, ((0, 64),))
    out_grad = centred(arg_keys[3], (TOKENS, QH * HD), 1.0, 6.0, ((0, 64), (1, 2)))
    doc_start = draw_doc_start(jax.random.fold_in(arg_keys[5], 71), 0)
    return {"queries": queries, "key_rows": key_rows, "value_rows": value_rows, "out_grad": out_grad, "doc_start": doc_start}


def attend_tile(query_block, key_block, value_block, grad_block, query_pos, key_pos, lower_bound, score_scale):
    query_f = query_block.astype(jnp.float32)
    key_f = key_block.astype(jnp.float32)
    value_f = value_block.astype(jnp.float32)
    grad_f = grad_block.astype(jnp.float32)
    scores = jnp.einsum('brgh,lgh->rgbl', query_f, key_f) * score_scale
    visible = (key_pos[None, :] >= lower_bound[:, None]) & (key_pos[None, :] <= query_pos[:, None]) & (query_pos[:, None] - key_pos[None, :] < WINDOW)
    masked = jnp.where(visible, scores, jnp.float32(-1e30))
    row_max = jnp.max(masked, axis=-1, keepdims=True)
    log_total = row_max + jnp.log(jnp.sum(jnp.exp(masked - row_max), axis=-1, keepdims=True))
    probs_exact = jnp.exp(masked - log_total)
    probs = probs_exact.astype(jnp.bfloat16)
    probs_f = probs.astype(jnp.float32)
    block_out = jnp.einsum('rgbl,lgh->brgh', probs_f, value_f).astype(jnp.bfloat16)
    row_delta = jnp.einsum('brgh,brgh->rgb', grad_f, block_out.astype(jnp.float32))[..., None]
    dprob = jnp.einsum('brgh,lgh->rgbl', grad_f, value_f)
    dscore = (probs_exact * (dprob - row_delta)).astype(jnp.bfloat16).astype(jnp.float32)
    query_part = (jnp.einsum('rgbl,lgh->brgh', dscore, key_f) * score_scale).astype(jnp.bfloat16)
    key_part = jnp.einsum('rgbl,brgh->lgh', dscore, query_f) * score_scale
    value_part = jnp.einsum('rgbl,brgh->lgh', probs_f, grad_f)
    return block_out, query_part, key_part, value_part


def reference(queries, key_rows, value_rows, out_grad, doc_start):
    block_rows = min(512, TOK_DEV)
    group_count = QH // KVH
    block_total = TOKENS // block_rows
    key_span = WINDOW + block_rows
    score_scale = HD ** -0.5
    zero_rows = jnp.zeros((WINDOW, KVH * HD), jnp.bfloat16)
    padded_keys = jnp.concatenate([zero_rows, key_rows], axis=0)
    padded_values = jnp.concatenate([zero_rows, value_rows], axis=0)
    positions = jnp.arange(TOKENS, dtype=jnp.int32)
    lower_all = jnp.maximum(doc_start, positions - WINDOW + 1)

    def scan_step(carried, block_index):
        key_acc, value_acc = carried
        start = (block_index * block_rows).astype(jnp.int32)
        query_block = lax.dynamic_slice_in_dim(queries, start, block_rows, 0).reshape(block_rows, group_count, KVH, HD)
        grad_block = lax.dynamic_slice_in_dim(out_grad, start, block_rows, 0).reshape(block_rows, group_count, KVH, HD)
        key_block = lax.dynamic_slice_in_dim(padded_keys, start, key_span, 0).reshape(key_span, KVH, HD)
        value_block = lax.dynamic_slice_in_dim(padded_values, start, key_span, 0).reshape(key_span, KVH, HD)
        query_pos = start + jnp.arange(block_rows, dtype=jnp.int32)
        key_pos = start - WINDOW + jnp.arange(key_span, dtype=jnp.int32)
        lower_bound = lax.dynamic_slice_in_dim(lower_all, start, block_rows, 0)
        block_out, query_part, key_part, value_part = attend_tile(query_block, key_block, value_block, grad_block, query_pos, key_pos, lower_bound, score_scale)
        old_keys = lax.dynamic_slice_in_dim(key_acc, start, key_span, 0)
        old_values = lax.dynamic_slice_in_dim(value_acc, start, key_span, 0)
        key_acc = lax.dynamic_update_slice_in_dim(key_acc, old_keys + key_part.reshape(key_span, KVH * HD), start, 0)
        value_acc = lax.dynamic_update_slice_in_dim(value_acc, old_values + value_part.reshape(key_span, KVH * HD), start, 0)
        return (key_acc, value_acc), (block_out.reshape(block_rows, QH * HD), query_part.reshape(block_rows, QH * HD))

    initial = (jnp.zeros((WINDOW + TOKENS, KVH * HD), jnp.float32), jnp.zeros((WINDOW + TOKENS, KVH * HD), jnp.float32))
    (key_acc, value_acc), (outs, query_parts) = lax.scan(scan_step, initial, jnp.arange(block_total, dtype=jnp.int32))
    attended = outs.reshape(TOKENS, QH * HD)
    query_grad = query_parts.reshape(TOKENS, QH * HD)
    return attended, query_grad, key_acc[WINDOW:].astype(jnp.bfloat16), value_acc[WINDOW:].astype(jnp.bfloat16)
```

```python
import functools

import jax
import jax.numpy as jnp
from jax import lax
from jax.experimental import pallas as pl
from jax.experimental.pallas import tpu as pltpu
from jax.sharding import PartitionSpec as P

KVH = 4
HD = 256
WINDOW = 1024
ROWS = 1024
QB = 256
SPAN = WINDOW + QB
SCALE = HD ** (-0.5)
NEG = -1e30 / SCALE
VMEM = 56 * 2**20


def nn(a, b):
    return jnp.dot(a, b, preferred_element_type=jnp.float32)


def block_grads(lo, q, do, ks, vs, kts, vts, base, with_out):
    qt = q.T
    dot_ = do.T
    s = nn(ks, qt)
    w = base + lax.broadcasted_iota(jnp.int32, (SPAN, QB), 0)
    hi = base + WINDOW + lax.broadcasted_iota(jnp.int32, (1, QB), 1)
    s = jnp.where((w >= lo) & (w <= hi), s, jnp.float32(NEG))
    m = jnp.max(s, axis=0, keepdims=True)
    e = jnp.exp((s - m) * jnp.float32(SCALE))
    p = e * (1.0 / jnp.sum(e, axis=0, keepdims=True))
    pb = p.astype(jnp.bfloat16)
    dp = nn(vs, dot_)
    if with_out:
        ot = nn(vts, pb).astype(jnp.bfloat16)
        delta = jnp.sum(dot_.astype(jnp.float32) * ot.astype(jnp.float32), axis=0, keepdims=True)
    else:
        delta = jnp.sum(p * dp, axis=0, keepdims=True)
    ds = (p * (dp - delta)).astype(jnp.bfloat16)
    if not with_out:
        return pb, ds, None, None
    dqt = (nn(kts, ds) * jnp.float32(SCALE)).astype(jnp.bfloat16)
    return pb, ds, ot.T, dqt.T


def attend_kernel(with_out, with_kv, n_alias, has_acc, g_ref, lo_ref, q_ref, do_ref, ko_ref, vo_ref, ekv_ref, *rest):
    rest = list(rest)
    acc_in = [rest.pop(0) for _ in range(2)] if has_acc else None
    rest = rest[n_alias:]
    if with_out:
        o_ref, dq_ref = rest.pop(0), rest.pop(0)
    if with_kv:
        early_ref, own_ref = rest.pop(0), rest.pop(0)
    kw, vw = rest.pop(0), rest.pop(0)
    if with_out:
        kt, vt = rest.pop(0), rest.pop(0)
    if with_kv:
        dk, dv = rest.pop(0), rest.pop(0)
    kw[:ROWS] = ekv_ref[:, :HD]
    vw[:ROWS] = ekv_ref[:, HD:]
    kw[ROWS:] = ko_ref[...]
    vw[ROWS:] = vo_ref[...]
    if with_out:
        kt[...] = kw[...].T
        vt[...] = vw[...].T
    if with_kv:
        if has_acc:
            dk[:ROWS] = acc_in[0][:, :HD]
            dv[:ROWS] = acc_in[0][:, HD:]
            dk[ROWS:] = acc_in[1][:, :HD]
            dv[ROWS:] = acc_in[1][:, HD:]
        else:
            dk[...] = jnp.zeros_like(dk)
            dv[...] = jnp.zeros_like(dv)
    for b in range(ROWS // QB):
        rows = slice(b * QB, (b + 1) * QB)
        span = slice(b * QB, b * QB + SPAN)
        q, do = q_ref[rows, :], do_ref[rows, :]
        pb, ds, o, dq = block_grads(
            lo_ref[:, rows], q, do, kw[span, :], vw[span, :],
            kt[:, span] if with_out else None, vt[:, span] if with_out else None,
            b * QB, with_out,
        )
        if with_out:
            o_ref[rows, :] = o
            dq_ref[rows, :] = dq
        if with_kv:
            dk[span, :] += nn(ds, q) * jnp.float32(SCALE)
            dv[span, :] += nn(pb, do)
    if with_kv:
        early_ref[:, :HD] = dk[:ROWS].astype(early_ref.dtype)
        early_ref[:, HD:] = dv[:ROWS].astype(early_ref.dtype)
        own_ref[:, :HD] = dk[ROWS:]
        own_ref[:, HD:] = dv[ROWS:]


def attend(g, lo, q, do, keys, values, ekv, *, with_out, with_kv, packed=False, outs=None, acc=None, early_dtype=jnp.float32):
    def at(index):
        return pl.BlockSpec((ROWS, HD), lambda i, s: (0, s[0]) if index is None else (0, index))

    def whole(shape):
        return pl.BlockSpec(shape, lambda i, s: (0, 0))

    qspecs = [at(0), at(1)] if packed else [at(None), at(None)]
    in_specs = [whole((1, ROWS))] + qspecs + [at(None), at(None), whole((ROWS, 2 * HD))]
    args = [lo, q, do, keys, values, ekv]
    if acc is not None:
        in_specs += [whole((ROWS, 2 * HD))] * 2
        args += list(acc)
    alias = {}
    n_alias = 0
    out_shapes, out_specs = [], []
    if with_out:
        if outs is not None:
            alias = {1 + len(args): 0, 2 + len(args): 1}
            in_specs += [pl.BlockSpec(memory_space=pl.ANY)] * 2
            args += list(outs)
            n_alias = 2
        out_shapes += [jax.ShapeDtypeStruct((ROWS, KVH * HD), jnp.bfloat16)] * 2
        out_specs += [at(None), at(None)]
    if with_kv:
        out_shapes += [
            jax.ShapeDtypeStruct((ROWS, 2 * HD), early_dtype),
            jax.ShapeDtypeStruct((ROWS, 2 * HD), jnp.float32),
        ]
        out_specs += [whole((ROWS, 2 * HD))] * 2
    scratch = [pltpu.VMEM((2 * ROWS, HD), jnp.bfloat16)] * 2
    if with_out:
        scratch += [pltpu.VMEM((HD, 2 * ROWS), jnp.bfloat16)] * 2
    if with_kv:
        scratch += [pltpu.VMEM((2 * ROWS, HD), jnp.float32)] * 2
    matmuls = 2 + 2 * with_out + 2 * with_kv
    return pl.pallas_call(
        functools.partial(attend_kernel, with_out, with_kv, n_alias, acc is not None),
        grid_spec=pltpu.PrefetchScalarGridSpec(
            num_scalar_prefetch=1, grid=(1,), in_specs=in_specs, out_specs=out_specs, scratch_shapes=scratch
        ),
        out_shape=out_shapes,
        input_output_aliases=alias,
        compiler_params=pltpu.CompilerParams(vmem_limit_bytes=VMEM),
        cost_estimate=pl.CostEstimate(
            flops=matmuls * 2 * ROWS * SPAN * HD, bytes_accessed=6 * 2**20, transcendentals=ROWS * SPAN
        ),
    )(g, *args)


def join_kernel(own_ref, got_ref, *rest):
    k_ref, v_ref = rest[-2:]
    k_ref[...] = (own_ref[:, :HD] + got_ref[:, :HD].astype(jnp.float32)).astype(jnp.bfloat16)
    v_ref[...] = (own_ref[:, HD:] + got_ref[:, HD:].astype(jnp.float32)).astype(jnp.bfloat16)


def join(own, got, column, outs=None):
    whole = pl.BlockSpec((ROWS, 2 * HD), lambda i: (0, 0))
    in_specs, args, alias = [whole, whole], [own, got], {}
    if outs is not None:
        in_specs += [pl.BlockSpec(memory_space=pl.ANY)] * 2
        args += list(outs)
        alias = {2: 0, 3: 1}
    return pl.pallas_call(
        join_kernel,
        grid=(1,),
        in_specs=in_specs,
        out_specs=[pl.BlockSpec((ROWS, HD), lambda i: (0, column))] * 2,
        out_shape=[jax.ShapeDtypeStruct((ROWS, 2 * HD), jnp.bfloat16)] * 2,
        input_output_aliases=alias,
        compiler_params=pltpu.CompilerParams(vmem_limit_bytes=VMEM),
        cost_estimate=pl.CostEstimate(flops=2**20, bytes_accessed=5 * 2**20, transcendentals=0),
    )(*args)


def pair_of(left, right, g):
    column = g * HD
    return jnp.concatenate(
        [lax.dynamic_slice_in_dim(left, column, HD, 1), lax.dynamic_slice_in_dim(right, column, HD, 1)], axis=1
    )


def local(queries, key_rows, value_rows, out_grad, doc_start):
    count = lax.axis_size("ctx")
    ctx, head = lax.axis_index("ctx"), lax.axis_index("head")
    own0, other0 = 2 * head, 2 - 2 * head
    crossing = ctx % 8 == 7

    def forward(value, cross):
        pairs = []
        for c in range(count - 1):
            for h in range(2):
                pairs.append((2 * c + (1 - h if cross and c % 8 == 7 else h), 2 * (c + 1) + h))
        return lax.ppermute(value, ("ctx", "head"), pairs)

    def backward(value):
        return lax.ppermute(value, "ctx", [(c + 1, c) for c in range(count - 1)])

    def swap(value):
        return lax.ppermute(value, "head", [(0, 1), (1, 0)])

    lo = jnp.maximum(doc_start - ctx * ROWS + ROWS, jnp.arange(1, ROWS + 1, dtype=jnp.int32)).reshape(1, ROWS)
    heads = [own0, own0 + 1, other0, other0 + 1]
    cross = [False, True, False, True]
    theirs = [other0, other0 + 1, own0, own0 + 1]
    ekv, pairs = [], []
    for k in range(4):
        g = jnp.where(crossing, theirs[k], heads[k]) if cross[k] else heads[k]
        ekv.append(forward(pair_of(key_rows, value_rows, g), cross[k]))
        if k < 2:
            pairs.append(swap(pair_of(queries, out_grad, theirs[k])))
    gs = [jnp.reshape(g, (1,)).astype(jnp.int32) for g in heads]
    outs, joined = None, None
    accs = []
    for k in range(2):
        *outs, early, own = attend(
            gs[k], lo, queries, out_grad, key_rows, value_rows, ekv[k], with_out=True, with_kv=True, outs=outs
        )
        early, own = attend(
            gs[k], lo, pairs[k], pairs[k], key_rows, value_rows, ekv[k], with_out=False, with_kv=True,
            packed=True, acc=(early, own), early_dtype=jnp.bfloat16,
        )
        accs.append((own, backward(early)))
        outs = tuple(attend(
            gs[k + 2], lo, queries, out_grad, key_rows, value_rows, ekv[k + 2], with_out=True, with_kv=False, outs=outs
        ))
    for k, (own, got) in enumerate(accs):
        joined = join(own, got, k, joined)
    return (outs[0], outs[1], joined[0], joined[1])


def solution(mesh):
    return jax.shard_map(
        local,
        mesh=mesh,
        in_specs=(P("ctx", "head"), P("ctx", None), P("ctx", None), P("ctx", "head"), P("ctx")),
        out_specs=(P("ctx", "head"), P("ctx", "head"), P("ctx", "head"), P("ctx", "head")),
        check_vma=False,
    )
```

```python
import functools

import jax
import jax.numpy as jnp
from jax import lax
from jax.experimental import pallas as pl
from jax.experimental.pallas import tpu as pltpu
from jax.sharding import PartitionSpec as P

KVH = 4
HD = 256
WINDOW = 1024
ROWS = 1024
QB = 256
SPAN = WINDOW + QB
SCALE = HD ** (-0.5)
NEG = -1e30 / SCALE
VMEM = 44 * 2**20
RELAY, CARRY = 4, 5
CHUNK = 640
LOG2E = 1.4426950408889634


def nn(a, b):
    return jnp.dot(a, b, preferred_element_type=jnp.float32)


def attend_kernel(with_out, with_kv, n_alias, has_acc, has_relay, g_ref, lo_ref, q_ref, do_ref, ko_ref, vo_ref, ekv_ref, *rest):
    rest = list(rest)
    relay_ref = rest.pop(0) if has_relay else None
    acc_ref = [rest.pop(0) for _ in range(2)] if has_acc else None
    rest = rest[n_alias:]
    if with_out:
        o_ref, dq_ref = rest.pop(0), rest.pop(0)
    if with_kv:
        early_ref, own_ref = rest.pop(0), rest.pop(0)
    kw, vw, s_ref, e_ref, dp_ref, ds_ref = [rest.pop(0) for _ in range(6)]
    if with_out:
        kt, vt = rest.pop(0), rest.pop(0)
    if with_kv:
        dk, dv = rest.pop(0), rest.pop(0)
    kw[:ROWS] = ekv_ref[:, :HD]
    vw[:ROWS] = ekv_ref[:, HD:]
    if has_relay:
        @pl.when(g_ref[RELAY] == 1)
        def _():
            kw[:ROWS] = relay_ref[:, :HD]
            vw[:ROWS] = relay_ref[:, HD:]

    kw[ROWS:] = ko_ref[...]
    vw[ROWS:] = vo_ref[...]
    if with_out:
        kt[...] = kw[...].T
        vt[...] = vw[...].T
    chunks = SPAN // CHUNK
    part = [slice(j * CHUNK, (j + 1) * CHUNK) for j in range(chunks)]
    blocks = ROWS // QB
    rows = [slice(b * QB, (b + 1) * QB) for b in range(blocks)]
    state = {}

    def keys_of(b, j):
        return slice(b * QB + j * CHUNK, b * QB + (j + 1) * CHUNK)

    def softmax(b):
        slot = b % 3
        qt = q_ref[rows[b], :].T
        lo = lo_ref[:, rows[b]] - b * QB
        w = lax.broadcasted_iota(jnp.int32, (CHUNK, QB), 0)
        hi = WINDOW + lax.broadcasted_iota(jnp.int32, (1, QB), 1)
        m = None
        for j in range(chunks):
            s = nn(kw[keys_of(b, j), :], qt)
            seen = w >= lo - j * CHUNK
            if (j + 1) * CHUNK > WINDOW:
                seen = seen & (w <= hi - j * CHUNK)
            s = jnp.where(seen, s, jnp.float32(NEG))
            s_ref[slot, part[j], :] = s
            mj = jnp.max(s, axis=0, keepdims=True)
            m = mj if m is None else jnp.maximum(m, mj)
        total = None
        for j in range(chunks):
            e = jnp.exp2((s_ref[slot, part[j], :] - m) * jnp.float32(SCALE * LOG2E))
            tj = jnp.sum(e, axis=0, keepdims=True)
            total = tj if total is None else total + tj
            e_ref[slot, part[j], :] = e.astype(jnp.bfloat16)
        inv = 1.0 / total
        dot_ = (do_ref[rows[b], :].T.astype(jnp.float32) * inv).astype(jnp.bfloat16)
        state[b] = (inv, dot_)

    def dscore(b):
        slot = b % 3
        dot_ = state[b][1]
        delta = None
        for j in range(chunks):
            dp = nn(vw[keys_of(b, j), :], dot_)
            dp_ref[slot, part[j], :] = dp
            dj = jnp.sum(e_ref[slot, part[j], :].astype(jnp.float32) * dp, axis=0, keepdims=True)
            delta = dj if delta is None else delta + dj
        for j in range(chunks):
            e = e_ref[slot, part[j], :].astype(jnp.float32)
            ds_ref[slot, part[j], :] = (e * (dp_ref[slot, part[j], :] - delta * state[b][0])).astype(jnp.bfloat16)

    def products(b):
        slot = b % 3
        inv, dot_ = state[b]
        span = slice(b * QB, b * QB + SPAN)
        e, ds = e_ref[slot], ds_ref[slot]
        if with_out:
            o_ref[rows[b], :] = (nn(vt[:, span], e) * inv).astype(jnp.bfloat16).T
            dq_ref[rows[b], :] = (nn(kt[:, span], ds) * jnp.float32(SCALE)).astype(jnp.bfloat16).T
        if with_kv:
            old = slice(b * QB, b * QB + (SPAN - QB if b else 0))
            gk, gv = nn(ds, q_ref[rows[b], :]), nn(e, dot_.T)
            if b == 0:
                dk[span, :] = gk
                dv[span, :] = gv
            else:
                fresh = slice(b * QB + SPAN - QB, b * QB + SPAN)
                dk[old, :] += gk[: SPAN - QB]
                dv[old, :] += gv[: SPAN - QB]
                dk[fresh, :] = gk[SPAN - QB :]
                dv[fresh, :] = gv[SPAN - QB :]

    for t in range(blocks + 2):
        if t < blocks:
            softmax(t)
        if 0 <= t - 1 < blocks:
            dscore(t - 1)
        if 0 <= t - 2:
            products(t - 2)
    if with_kv:
        for half, ref in ((slice(0, ROWS), early_ref), (slice(ROWS, 2 * ROWS), own_ref)):
            k, v = dk[half] * jnp.float32(SCALE), dv[half]
            if has_acc:
                old = acc_ref[0 if ref is early_ref else 1]
                k, v = k + old[:, :HD].astype(jnp.float32), v + old[:, HD:].astype(jnp.float32)
            ref[:, :HD] = k.astype(ref.dtype)
            ref[:, HD:] = v.astype(ref.dtype)


def attend(heads, k, lo, q, do, keys, values, ekv, *, with_out, with_kv, relay=None, packed=False, outs=None, acc=None):
    def at(index):
        return pl.BlockSpec((ROWS, HD), lambda i, s: (0, s[k]) if index is None else (0, index))

    def whole(shape):
        return pl.BlockSpec(shape, lambda i, s: (0, 0))

    def block(index):
        return pl.BlockSpec((ROWS, 2 * HD), lambda i, s: (0, index))

    qspecs = [at(0), at(1)] if packed else [at(None), at(None)]
    in_specs = [whole((1, ROWS))] + qspecs + [at(None), at(None), block(ekv[1])]
    args = [lo, q, do, keys, values, ekv[0]]
    if relay is not None:
        in_specs.append(whole((ROWS, 2 * HD)))
        args.append(relay)
    if acc is not None:
        in_specs += [whole((ROWS, 2 * HD))] * 2
        args += list(acc)
    alias = {}
    n_alias = 0
    out_shapes, out_specs = [], []
    if with_out:
        if outs is not None:
            alias = {1 + len(args): 0, 2 + len(args): 1}
            in_specs += [pl.BlockSpec(memory_space=pl.ANY)] * 2
            args += list(outs)
            n_alias = 2
        out_shapes += [jax.ShapeDtypeStruct((ROWS, KVH * HD), jnp.bfloat16)] * 2
        out_specs += [at(None), at(None)]
    if with_kv:
        out_shapes += [
            jax.ShapeDtypeStruct((ROWS, 2 * HD), jnp.bfloat16),
            jax.ShapeDtypeStruct((ROWS, 2 * HD), jnp.bfloat16),
        ]
        out_specs += [whole((ROWS, 2 * HD))] * 2
    scratch = [pltpu.VMEM((2 * ROWS, HD), jnp.bfloat16)] * 2
    scratch += [pltpu.VMEM((3, SPAN, QB), dtype) for dtype in (jnp.float32, jnp.bfloat16, jnp.float32, jnp.bfloat16)]
    if with_out:
        scratch += [pltpu.VMEM((HD, 2 * ROWS), jnp.bfloat16)] * 2
    if with_kv:
        scratch += [pltpu.VMEM((2 * ROWS, HD), jnp.float32)] * 2
    matmuls = 2 + 2 * with_out + 2 * with_kv
    return pl.pallas_call(
        functools.partial(attend_kernel, with_out, with_kv, n_alias, acc is not None, relay is not None),
        grid_spec=pltpu.PrefetchScalarGridSpec(
            num_scalar_prefetch=1, grid=(1,), in_specs=in_specs, out_specs=out_specs, scratch_shapes=scratch
        ),
        out_shape=out_shapes,
        input_output_aliases=alias,
        compiler_params=pltpu.CompilerParams(vmem_limit_bytes=VMEM),
        cost_estimate=pl.CostEstimate(
            flops=matmuls * 2 * ROWS * SPAN * HD, bytes_accessed=6 * 2**20, transcendentals=ROWS * SPAN
        ),
    )(heads, *args)


def join_kernel(plain, flagged, when, split, s_ref, *refs):
    parts, rest = refs[: plain + flagged], refs[plain + flagged :]
    for half in range(2):
        columns = slice(half * HD, (half + 1) * HD)
        total = parts[0][:, columns].astype(jnp.float32)
        for part in parts[1:plain]:
            total = total + part[:, columns].astype(jnp.float32)
        if flagged:
            last = parts[plain][:, columns].astype(jnp.float32)
            total = total + jnp.where(s_ref[CARRY] == when, last, 0.0)
        if split:
            rest[half - 2][...] = total.astype(jnp.bfloat16)
        else:
            rest[-1][:, columns] = total.astype(jnp.bfloat16)


def join(heads, terms, last=None, when=0, column=None, outs=None):
    whole = pl.BlockSpec((ROWS, 2 * HD), lambda i, s: (0, 0))
    args = list(terms) + ([] if last is None else [last])
    in_specs, alias = [whole] * len(args), {}
    split = column is not None
    count = len(args)
    if outs is not None:
        in_specs += [pl.BlockSpec(memory_space=pl.ANY)] * 2
        alias = {1 + count: 0, 2 + count: 1}
        args += list(outs)
    out = jax.ShapeDtypeStruct((ROWS, 2 * HD), jnp.bfloat16)
    return pl.pallas_call(
        functools.partial(join_kernel, len(terms), last is not None, when, split),
        grid_spec=pltpu.PrefetchScalarGridSpec(
            num_scalar_prefetch=1, grid=(1,), in_specs=in_specs,
            out_specs=[pl.BlockSpec((ROWS, HD), lambda i, s: (0, column))] * 2 if split else [whole],
        ),
        out_shape=[out] * (2 if split else 1),
        input_output_aliases=alias,
        compiler_params=pltpu.CompilerParams(vmem_limit_bytes=VMEM),
        cost_estimate=pl.CostEstimate(flops=2**20, bytes_accessed=3 * 2**20, transcendentals=0),
    )(heads, *args)


def pack_kernel(groups, g_ref, *refs):
    heads = [k for ks in groups for k in ks]
    pairs = len(heads)
    held, sems = refs[-2:]
    outs = refs[2 * pairs : -2]
    ins, done = [], []
    for i, k in enumerate(heads):
        columns = pl.ds(pl.multiple_of(g_ref[k] * HD, HD), HD)
        for half in range(2):
            ins.append(
                pltpu.make_async_copy(
                    refs[2 * i + half].at[:, columns],
                    held.at[:, pl.ds((2 * i + half) * HD, HD)],
                    sems.at[2 * i + half],
                )
            )
    first = 0
    for j, ks in enumerate(groups):
        done.append(
            pltpu.make_async_copy(
                held.at[:, pl.ds(2 * first * HD, 2 * len(ks) * HD)], outs[j], sems.at[2 * pairs + j]
            )
        )
        first += len(ks)
    for copy in ins:
        copy.start()
    first = 0
    for j, ks in enumerate(groups):
        for copy in ins[2 * first : 2 * (first + len(ks))]:
            copy.wait()
        done[j].start()
        first += len(ks)
    for copy in done:
        copy.wait()


def pack(heads, *groups):
    ks = [[k for _, _, k in group] for group in groups]
    arrays = [x for group in groups for left, right, _ in group for x in (left, right)]
    pairs = len(arrays) // 2
    return pl.pallas_call(
        functools.partial(pack_kernel, ks),
        grid_spec=pltpu.PrefetchScalarGridSpec(
            num_scalar_prefetch=1, grid=(1,), in_specs=[pl.BlockSpec(memory_space=pl.ANY)] * len(arrays),
            out_specs=[pl.BlockSpec(memory_space=pl.ANY)] * len(ks),
            scratch_shapes=[
                pltpu.VMEM((ROWS, pairs * 2 * HD), jnp.bfloat16),
                pltpu.SemaphoreType.DMA((2 * pairs + len(ks),)),
            ],
        ),
        out_shape=[jax.ShapeDtypeStruct((ROWS, 2 * HD * len(k)), jnp.bfloat16) for k in ks],
        compiler_params=pltpu.CompilerParams(vmem_limit_bytes=60 * 2**20),
        cost_estimate=pl.CostEstimate(flops=0, bytes_accessed=pairs * 2**21, transcendentals=0),
    )(heads, *arrays)


def local(queries, key_rows, value_rows, out_grad, doc_start):
    count = lax.axis_size("ctx")
    ctx, head = lax.axis_index("ctx"), lax.axis_index("head")
    mine, theirs = 2 * head, 2 - 2 * head
    heads = jnp.stack([mine, mine + 1, theirs, theirs + 1, ctx % 8 == 0, ctx % 8 == 7]).astype(jnp.int32)
    inner = [c for c in range(count - 1) if c % 8 != 7]
    carry = [c for c in range(count - 1) if c % 8 == 7]
    both = range(2)

    def permute(value, pairs):
        return lax.ppermute(value, ("ctx", "head"), [(2 * c + h, 2 * d + i) for c, h, d, i in pairs])

    def forward(value, straight):
        return permute(value, [(c, h, c + 1, h) for c in (range(count - 1) if straight else inner) for h in both])

    def relay(value):
        first = permute(value, [(c, h, c + 7, 1 - h) for c in carry for h in both])
        return permute(first, [(c + 7, h, c + 1, h) for c in carry for h in both])

    def backward(value):
        return permute(value, [(c + 1, h, c, h) for c in range(count - 1) for h in both])

    def backward_other(value):
        return permute(value, [(c + 1, h, c, 1 - h if c % 8 == 7 else h) for c in range(count - 1) for h in both])

    def swap(value):
        return lax.ppermute(value, "head", [(0, 1), (1, 0)])

    lo = jnp.maximum(doc_start - ctx * ROWS + ROWS, jnp.arange(1, ROWS + 1, dtype=jnp.int32)).reshape(1, ROWS)
    kv, qg = (key_rows, value_rows), (queries, out_grad)
    (sent_b,) = pack(heads, [(*kv, 3)])
    kv_b = forward(sent_b, True)
    sent_c, swap_a, sent_da = pack(heads, [(*kv, 0)], [(*qg, 2)], [(*kv, 1), (*kv, 2)])
    kv_c = forward(sent_c, True)
    pair = swap(swap_a)
    kv_da = forward(sent_da, True)
    own = (queries, out_grad, key_rows, value_rows)
    *outs, early_b, own_b = attend(heads, 3, lo, *own, (kv_b, 0), with_out=True, with_kv=True)
    got_b = backward_other(early_b)
    *outs, early_c, own_c = attend(heads, 0, lo, *own, (kv_c, 0), with_out=True, with_kv=True, outs=outs)
    got_b, outs = lax.optimization_barrier((got_b, outs))
    (sum_b,) = join(heads, [own_b], got_b, 0)
    other_d = swap(sum_b)
    pair, sum_b = lax.optimization_barrier((pair, sum_b))
    early_c, own_c = attend(
        heads, 0, lo, pair, pair, key_rows, value_rows, (kv_c, 0), with_out=False, with_kv=True,
        packed=True, acc=(early_c, own_c),
    )
    got_c = backward(early_c)
    outs, own_c = lax.optimization_barrier((outs, own_c))
    *outs, early_d, own_d = attend(heads, 1, lo, *own, (kv_da, 0), with_out=True, with_kv=True, outs=outs)
    got_d = backward(early_d)
    outs = attend(heads, 2, lo, *own, (kv_da, 1), with_out=True, with_kv=False, outs=outs)
    joined = join(heads, [own_c, got_c], column=0)
    joined = join(heads, [own_d, got_d, other_d], got_b, 1, column=1, outs=joined)
    return (outs[0], outs[1], joined[0], joined[1])


def solution(mesh):
    return jax.shard_map(
        local,
        mesh=mesh,
        in_specs=(P("ctx", "head"), P("ctx", None), P("ctx", None), P("ctx", "head"), P("ctx")),
        out_specs=(P("ctx", "head"), P("ctx", "head"), P("ctx", "head"), P("ctx", "head")),
        check_vma=False,
    )
```

```python
import functools

import jax
import jax.numpy as jnp
from jax import lax
from jax.experimental import pallas as pl
from jax.experimental.pallas import tpu as pltpu
from jax.sharding import PartitionSpec as P

KVH = 4
HD = 256
WINDOW = 1024
ROWS = 1024
QB = 256
SPAN = WINDOW + QB
SCALE = HD ** (-0.5)
NEG = -1e30 / SCALE
VMEM = 44 * 2**20
RELAY, CARRY = 4, 5
CHUNK = 640
LOG2E = 1.4426950408889634


def nn(a, b):
    return jnp.dot(a, b, preferred_element_type=jnp.float32)


def attend_kernel(with_out, with_kv, n_alias, has_acc, has_relay, g_ref, lo_ref, q_ref, do_ref, ko_ref, vo_ref, ekv_ref, *rest):
    rest = list(rest)
    relay_ref = rest.pop(0) if has_relay else None
    acc_ref = [rest.pop(0) for _ in range(2)] if has_acc else None
    rest = rest[n_alias:]
    if with_out:
        o_ref, dq_ref = rest.pop(0), rest.pop(0)
    if with_kv:
        early_ref, own_ref = rest.pop(0), rest.pop(0)
    kw, vw, s_ref, e_ref, dp_ref, ds_ref = [rest.pop(0) for _ in range(6)]
    if with_out:
        kt, vt = rest.pop(0), rest.pop(0)
    if with_kv:
        dk, dv = rest.pop(0), rest.pop(0)
    kw[:ROWS] = ekv_ref[:, :HD]
    vw[:ROWS] = ekv_ref[:, HD:]
    if has_relay:
        @pl.when(g_ref[RELAY] == 1)
        def _():
            kw[:ROWS] = relay_ref[:, :HD]
            vw[:ROWS] = relay_ref[:, HD:]

    kw[ROWS:] = ko_ref[...]
    vw[ROWS:] = vo_ref[...]
    if with_out:
        kt[...] = kw[...].T
        vt[...] = vw[...].T
    chunks = SPAN // CHUNK
    part = [slice(j * CHUNK, (j + 1) * CHUNK) for j in range(chunks)]
    blocks = ROWS // QB
    rows = [slice(b * QB, (b + 1) * QB) for b in range(blocks)]
    state = {}

    def keys_of(b, j):
        return slice(b * QB + j * CHUNK, b * QB + (j + 1) * CHUNK)

    def softmax(b):
        slot = b % 3
        qt = q_ref[rows[b], :].T
        lo = lo_ref[:, rows[b]] - b * QB
        w = lax.broadcasted_iota(jnp.int32, (CHUNK, QB), 0)
        hi = WINDOW + lax.broadcasted_iota(jnp.int32, (1, QB), 1)
        m = None
        for j in range(chunks):
            s = nn(kw[keys_of(b, j), :], qt)
            seen = w >= lo - j * CHUNK
            if (j + 1) * CHUNK > WINDOW:
                seen = seen & (w <= hi - j * CHUNK)
            s = jnp.where(seen, s, jnp.float32(NEG))
            s_ref[slot, part[j], :] = s
            mj = jnp.max(s, axis=0, keepdims=True)
            m = mj if m is None else jnp.maximum(m, mj)
        total = None
        for j in range(chunks):
            e = jnp.exp2((s_ref[slot, part[j], :] - m) * jnp.float32(SCALE * LOG2E))
            tj = jnp.sum(e, axis=0, keepdims=True)
            total = tj if total is None else total + tj
            e_ref[slot, part[j], :] = e.astype(jnp.bfloat16)
        inv = 1.0 / total
        dot_ = (do_ref[rows[b], :].T.astype(jnp.float32) * inv).astype(jnp.bfloat16)
        state[b] = (inv, dot_)

    def dscore(b):
        slot = b % 3
        dot_ = state[b][1]
        delta = None
        for j in range(chunks):
            dp = nn(vw[keys_of(b, j), :], dot_)
            dp_ref[slot, part[j], :] = dp
            dj = jnp.sum(e_ref[slot, part[j], :].astype(jnp.float32) * dp, axis=0, keepdims=True)
            delta = dj if delta is None else delta + dj
        for j in range(chunks):
            e = e_ref[slot, part[j], :].astype(jnp.float32)
            ds_ref[slot, part[j], :] = (e * (dp_ref[slot, part[j], :] - delta * state[b][0])).astype(jnp.bfloat16)

    def products(b):
        slot = b % 3
        inv, dot_ = state[b]
        span = slice(b * QB, b * QB + SPAN)
        e, ds = e_ref[slot], ds_ref[slot]
        if with_out:
            o_ref[rows[b], :] = (nn(vt[:, span], e) * inv).astype(jnp.bfloat16).T
            dq_ref[rows[b], :] = (nn(kt[:, span], ds) * jnp.float32(SCALE)).astype(jnp.bfloat16).T
        if with_kv:
            old = slice(b * QB, b * QB + (SPAN - QB if b else 0))
            gk, gv = nn(ds, q_ref[rows[b], :]), nn(e, dot_.T)
            if b == 0:
                dk[span, :] = gk
                dv[span, :] = gv
            else:
                fresh = slice(b * QB + SPAN - QB, b * QB + SPAN)
                dk[old, :] += gk[: SPAN - QB]
                dv[old, :] += gv[: SPAN - QB]
                dk[fresh, :] = gk[SPAN - QB :]
                dv[fresh, :] = gv[SPAN - QB :]

    for t in range(blocks + 2):
        if t < blocks:
            softmax(t)
        if 0 <= t - 1 < blocks:
            dscore(t - 1)
        if 0 <= t - 2:
            products(t - 2)
    if with_kv:
        for half, ref in ((slice(0, ROWS), early_ref), (slice(ROWS, 2 * ROWS), own_ref)):
            k, v = dk[half] * jnp.float32(SCALE), dv[half]
            if has_acc:
                old = acc_ref[0 if ref is early_ref else 1]
                k, v = k + old[:, :HD].astype(jnp.float32), v + old[:, HD:].astype(jnp.float32)
            ref[:, :HD] = k.astype(ref.dtype)
            ref[:, HD:] = v.astype(ref.dtype)


def attend(heads, k, lo, q, do, keys, values, ekv, *, with_out, with_kv, relay=None, packed=False, outs=None, acc=None):
    def at(index):
        return pl.BlockSpec((ROWS, HD), lambda i, s: (0, s[k]) if index is None else (0, index))

    def whole(shape):
        return pl.BlockSpec(shape, lambda i, s: (0, 0))

    def block(index):
        return pl.BlockSpec((ROWS, 2 * HD), lambda i, s: (0, index))

    qspecs = [at(0), at(1)] if packed else [at(None), at(None)]
    in_specs = [whole((1, ROWS))] + qspecs + [at(None), at(None), block(ekv[1])]
    args = [lo, q, do, keys, values, ekv[0]]
    if relay is not None:
        in_specs.append(whole((ROWS, 2 * HD)))
        args.append(relay)
    if acc is not None:
        in_specs += [whole((ROWS, 2 * HD))] * 2
        args += list(acc)
    alias = {}
    n_alias = 0
    out_shapes, out_specs = [], []
    if with_out:
        if outs is not None:
            alias = {1 + len(args): 0, 2 + len(args): 1}
            in_specs += [pl.BlockSpec(memory_space=pl.ANY)] * 2
            args += list(outs)
            n_alias = 2
        out_shapes += [jax.ShapeDtypeStruct((ROWS, KVH * HD), jnp.bfloat16)] * 2
        out_specs += [at(None), at(None)]
    if with_kv:
        out_shapes += [
            jax.ShapeDtypeStruct((ROWS, 2 * HD), jnp.bfloat16),
            jax.ShapeDtypeStruct((ROWS, 2 * HD), jnp.bfloat16),
        ]
        out_specs += [whole((ROWS, 2 * HD))] * 2
    scratch = [pltpu.VMEM((2 * ROWS, HD), jnp.bfloat16)] * 2
    scratch += [pltpu.VMEM((3, SPAN, QB), dtype) for dtype in (jnp.float32, jnp.bfloat16, jnp.float32, jnp.bfloat16)]
    if with_out:
        scratch += [pltpu.VMEM((HD, 2 * ROWS), jnp.bfloat16)] * 2
    if with_kv:
        scratch += [pltpu.VMEM((2 * ROWS, HD), jnp.float32)] * 2
    matmuls = 2 + 2 * with_out + 2 * with_kv
    return pl.pallas_call(
        functools.partial(attend_kernel, with_out, with_kv, n_alias, acc is not None, relay is not None),
        grid_spec=pltpu.PrefetchScalarGridSpec(
            num_scalar_prefetch=1, grid=(1,), in_specs=in_specs, out_specs=out_specs, scratch_shapes=scratch
        ),
        out_shape=out_shapes,
        input_output_aliases=alias,
        compiler_params=pltpu.CompilerParams(vmem_limit_bytes=60 * 2**20 if k == 3 else VMEM),
        cost_estimate=pl.CostEstimate(
            flops=matmuls * 2 * ROWS * SPAN * HD, bytes_accessed=6 * 2**20, transcendentals=ROWS * SPAN
        ),
    )(heads, *args)


def join_kernel(plain, flagged, when, split, s_ref, *refs):
    parts, rest = refs[: plain + flagged], refs[plain + flagged :]
    for half in range(2):
        columns = slice(half * HD, (half + 1) * HD)
        total = parts[0][:, columns].astype(jnp.float32)
        for part in parts[1:plain]:
            total = total + part[:, columns].astype(jnp.float32)
        if flagged:
            last = parts[plain][:, columns].astype(jnp.float32)
            total = total + jnp.where(s_ref[CARRY] == when, last, 0.0)
        if split:
            rest[half - 2][...] = total.astype(jnp.bfloat16)
        else:
            rest[-1][:, columns] = total.astype(jnp.bfloat16)


def join(heads, terms, last=None, when=0, column=None, outs=None):
    whole = pl.BlockSpec((ROWS, 2 * HD), lambda i, s: (0, 0))
    args = list(terms) + ([] if last is None else [last])
    in_specs, alias = [whole] * len(args), {}
    split = column is not None
    count = len(args)
    if outs is not None:
        in_specs += [pl.BlockSpec(memory_space=pl.ANY)] * 2
        alias = {1 + count: 0, 2 + count: 1}
        args += list(outs)
    out = jax.ShapeDtypeStruct((ROWS, 2 * HD), jnp.bfloat16)
    return pl.pallas_call(
        functools.partial(join_kernel, len(terms), last is not None, when, split),
        grid_spec=pltpu.PrefetchScalarGridSpec(
            num_scalar_prefetch=1, grid=(1,), in_specs=in_specs,
            out_specs=[pl.BlockSpec((ROWS, HD), lambda i, s: (0, column))] * 2 if split else [whole],
        ),
        out_shape=[out] * (2 if split else 1),
        input_output_aliases=alias,
        compiler_params=pltpu.CompilerParams(vmem_limit_bytes=VMEM),
        cost_estimate=pl.CostEstimate(flops=2**20, bytes_accessed=3 * 2**20, transcendentals=0),
    )(heads, *args)


def pack_kernel(groups, g_ref, *refs):
    heads = [k for ks in groups for k in ks]
    pairs = len(heads)
    held, sems = refs[-2:]
    outs = refs[2 * pairs : -2]
    ins, done = [], []
    for i, k in enumerate(heads):
        columns = pl.ds(pl.multiple_of(g_ref[k] * HD, HD), HD)
        for half in range(2):
            ins.append(
                pltpu.make_async_copy(
                    refs[2 * i + half].at[:, columns],
                    held.at[:, pl.ds((2 * i + half) * HD, HD)],
                    sems.at[2 * i + half],
                )
            )
    first = 0
    for j, ks in enumerate(groups):
        done.append(
            pltpu.make_async_copy(
                held.at[:, pl.ds(2 * first * HD, 2 * len(ks) * HD)], outs[j], sems.at[2 * pairs + j]
            )
        )
        first += len(ks)
    for copy in ins:
        copy.start()
    first = 0
    for j, ks in enumerate(groups):
        for copy in ins[2 * first : 2 * (first + len(ks))]:
            copy.wait()
        done[j].start()
        first += len(ks)
    for copy in done:
        copy.wait()


def pack(heads, *groups):
    ks = [[k for _, _, k in group] for group in groups]
    arrays = [x for group in groups for left, right, _ in group for x in (left, right)]
    pairs = len(arrays) // 2
    return pl.pallas_call(
        functools.partial(pack_kernel, ks),
        grid_spec=pltpu.PrefetchScalarGridSpec(
            num_scalar_prefetch=1, grid=(1,), in_specs=[pl.BlockSpec(memory_space=pl.ANY)] * len(arrays),
            out_specs=[pl.BlockSpec(memory_space=pl.ANY)] * len(ks),
            scratch_shapes=[
                pltpu.VMEM((ROWS, pairs * 2 * HD), jnp.bfloat16),
                pltpu.SemaphoreType.DMA((2 * pairs + len(ks),)),
            ],
        ),
        out_shape=[jax.ShapeDtypeStruct((ROWS, 2 * HD * len(k)), jnp.bfloat16) for k in ks],
        compiler_params=pltpu.CompilerParams(vmem_limit_bytes=60 * 2**20),
        cost_estimate=pl.CostEstimate(flops=0, bytes_accessed=pairs * 2**21, transcendentals=0),
    )(heads, *arrays)


def local(queries, key_rows, value_rows, out_grad, doc_start):
    count = lax.axis_size("ctx")
    ctx, head = lax.axis_index("ctx"), lax.axis_index("head")
    mine, theirs = 2 * head, 2 - 2 * head
    heads = jnp.stack([mine, mine + 1, theirs, theirs + 1, ctx % 8 == 0, ctx % 8 == 7]).astype(jnp.int32)
    inner = [c for c in range(count - 1) if c % 8 != 7]
    carry = [c for c in range(count - 1) if c % 8 == 7]
    both = range(2)

    def permute(value, pairs):
        return lax.ppermute(value, ("ctx", "head"), [(2 * c + h, 2 * d + i) for c, h, d, i in pairs])

    def forward(value, straight):
        return permute(value, [(c, h, c + 1, h) for c in (range(count - 1) if straight else inner) for h in both])

    def relay(value):
        first = permute(value, [(c, h, c + 7, 1 - h) for c in carry for h in both])
        return permute(first, [(c + 7, h, c + 1, h) for c in carry for h in both])

    def backward(value):
        return permute(value, [(c + 1, h, c, h) for c in range(count - 1) for h in both])

    def backward_other(value):
        return permute(value, [(c + 1, h, c, 1 - h if c % 8 == 7 else h) for c in range(count - 1) for h in both])

    def swap(value):
        return lax.ppermute(value, "head", [(0, 1), (1, 0)])

    lo = jnp.maximum(doc_start - ctx * ROWS + ROWS, jnp.arange(1, ROWS + 1, dtype=jnp.int32)).reshape(1, ROWS)
    kv, qg = (key_rows, value_rows), (queries, out_grad)
    (sent_b,) = pack(heads, [(*kv, 3)])
    kv_b = forward(sent_b, True)
    sent_c, swap_a, sent_da = pack(heads, [(*kv, 0)], [(*qg, 2)], [(*kv, 1), (*kv, 2)])
    kv_c = forward(sent_c, True)
    pair = swap(swap_a)
    kv_da = forward(sent_da, True)
    own = (queries, out_grad, key_rows, value_rows)
    *outs, early_b, own_b = attend(heads, 3, lo, *own, (kv_b, 0), with_out=True, with_kv=True)
    got_b = backward_other(early_b)
    *outs, early_c, own_c = attend(heads, 0, lo, *own, (kv_c, 0), with_out=True, with_kv=True, outs=outs)
    got_b, outs = lax.optimization_barrier((got_b, outs))
    (sum_b,) = join(heads, [own_b], got_b, 0)
    other_d = swap(sum_b)
    pair, sum_b = lax.optimization_barrier((pair, sum_b))
    early_c, own_c = attend(
        heads, 0, lo, pair, pair, key_rows, value_rows, (kv_c, 0), with_out=False, with_kv=True,
        packed=True, acc=(early_c, own_c),
    )
    got_c = backward(early_c)
    outs, own_c = lax.optimization_barrier((outs, own_c))
    *outs, early_d, own_d = attend(heads, 1, lo, *own, (kv_da, 0), with_out=True, with_kv=True, outs=outs)
    got_d = backward(early_d)
    outs = attend(heads, 2, lo, *own, (kv_da, 1), with_out=True, with_kv=False, outs=outs)
    joined = join(heads, [own_c, got_c], column=0)
    joined = join(heads, [own_d, got_d, other_d], got_b, 1, column=1, outs=joined)
    return (outs[0], outs[1], joined[0], joined[1])


def solution(mesh):
    return jax.shard_map(
        local,
        mesh=mesh,
        in_specs=(P("ctx", "head"), P("ctx", None), P("ctx", None), P("ctx", "head"), P("ctx")),
        out_specs=(P("ctx", "head"), P("ctx", "head"), P("ctx", "head"), P("ctx", "head")),
        check_vma=False,
    )
```
